32 devices in a mesh: groups: 2 (over x), rep: 16 (over z, y, core).
Axes of the slice: x: 2, y: 2, z: 4, core: 2. Of those that a mesh axis runs over, the one named last changes fastest.
Arguments:
- features: float32 [24576, 256], P(('groups', 'rep')), parts along dimension 0, may hold values from -6 to 6
- weight: bfloat16 [256, 256], replicated, may hold values from -0.375 to 0.375
- adjacency: bfloat16 [192, 60, 128, 128], P(('groups', 'rep')), parts along dimension 0, may hold values from -0.0625 to 0.0625
- col_tiles: int32 [192, 60], P(('groups', 'rep')), parts along dimension 0, may hold values from 0 to 95, as said below
Outputs:
- hidden_out: float32 [24576, 256], P(('groups', 'rep')), parts along dimension 0
The draws below stay inside these ranges and needn't reach their ends.
There are 2 independent parts, one for each index of `groups`. The reference program is written for one: setup_inputs(seed, part) draws one part's arguments, and reference() takes and returns one part's arrays. A program takes and returns all parts, laid end to end along the dimension named above; an argument that names none is the same for every part. Nothing has to cross between parts.
Inputs may be any that keep to these rules, and one draw needn't show every extreme that they name: `col_tiles`: the 60 column tiles of one row tile differ. The row tiles of one device, 6 of them, name exactly 4 distinct tiles among the 6 row tiles of every device, its own included.
All inputs are finite; a program needn't handle non-finite values.
Results may differ from the reference program's by a relative error of at most 0.0041.
Values may be sent and summed in bfloat16 or wider, within the bound.
A program may use at most 128 MiB of HBM per device.

```python
import jax
import jax.numpy as jnp
from jax import lax

FEAT = 256
TILE = 128
NONZERO = 60
TILES_DEV = 6
CAP = 4
ROW_TILES = 96
NODES = 12288


def draw_col_tiles(key, part):
    key = jax.random.fold_in(key, 7)
    owners = ROW_TILES // TILES_DEV
    span = owners * CAP
    first, second = jax.random.split(key)
    noise = jax.random.randint(first, (owners, owners, TILES_DEV), 0, 1 << 20) * TILES_DEV + jnp.arange(TILES_DEV, dtype=jnp.int32)
    chosen = jnp.argsort(noise, axis=-1)[:, :, :CAP].astype(jnp.int32)
    needed = (chosen + jnp.arange(owners, dtype=jnp.int32)[None, :, None] * TILES_DEV).reshape(owners, span)
    order_noise = jax.random.randint(second, (owners, span), 0, 1 << 20) * span + jnp.arange(span, dtype=jnp.int32)
    ordering = jnp.argsort(order_noise, axis=-1).astype(jnp.int32)
    spots = jnp.arange(TILES_DEV * NONZERO, dtype=jnp.int32) % span
    picked = jnp.take_along_axis(needed, ordering[:, spots], axis=1)
    return picked.reshape(ROW_TILES, NONZERO).astype(jnp.int32)


def steps_of(rng, shape, cuts, low, top_value):
    gain, own = 1.0, jax.random.fold_in(rng, 6)
    for dim, shards_of in cuts:
        draws = jnp.exp(jax.random.uniform(jax.random.fold_in(own, dim), (shards_of,), jnp.float32, low / len(cuts), top_value / len(cuts)))
        gain = gain * jnp.repeat(draws, shape[dim] // shards_of).reshape([-1 if axis == dim else 1 for axis in range(len(shape))])
    return gain


def normal_values(stream_key, dims, scale, most, cuts=(), kind=jnp.bfloat16):
    values = jax.random.normal(stream_key, dims, jnp.float32) * scale
    if len(cuts) > 0:
        values = steps_of(stream_key, dims, cuts, -0.22, 0.18) * values
    return jnp.clip(values, min=-most, max=most).astype(kind)


def setup_inputs(seed: int = 0, part: int = 0) -> dict:
    streams_of = jax.random.split(jax.random.key(seed), 5)
    part_keys = jax.random.split(jax.random.fold_in(streams_of[4], part), 5)
    features = normal_values(part_keys[0], (NODES, FEAT), 1.0, 6.0, ((0, 16),), jnp.float32)
    weight = normal_values(streams_of[1], (FEAT, FEAT), FEAT ** -0.5, 0.375)
    adjacency = normal_values(part_keys[2], (ROW_TILES, NONZERO, TILE, TILE), (NONZERO * TILE) ** -0.5, 0.0625, ((0, 16),))
    col_tiles = draw_col_tiles(jax.random.fold_in(jax.random.fold_in(streams_of[4], part), 71), part)
    return dict(features=features, weight=weight, adjacency=adjacency, col_tiles=col_tiles)


def reference(features, weight, adjacency, col_tiles):
    projected = jnp.dot(features.astype(jnp.bfloat16), weight, preferred_element_type=jnp.float32).astype(jnp.bfloat16)
    stacked = projected.reshape(ROW_TILES, TILE, FEAT)

    def one_panel(inputs):
        panel_tiles, named_cols = inputs
        picked = stacked[named_cols.astype(jnp.int32)].astype(jnp.float32)
        return jnp.einsum('kab,kbf->af', panel_tiles.astype(jnp.float32), picked)

    summed = lax.map(one_panel, (adjacency, col_tiles))
    return jnp.maximum(summed, 0.0).reshape(NODES, FEAT)
```

```python
import functools

import jax
import jax.numpy as jnp
from jax import lax
from jax.experimental import pallas as pl
from jax.experimental.pallas import tpu as pltpu
from jax.sharding import PartitionSpec as P

MESH = pl.DeviceIdType.MESH


def kernel(depth, tiles, feat_ref, weight_ref, slot_ref, adj_ref, out_ref,
           held, adj, adj_sem, recv_sem, z_sem, y_sem, c_sem):
    rep = depth * 4
    every = rep * tiles
    rows = held.shape[1]
    stored = adj_ref.shape[0]
    last = tiles - 1
    me = lax.axis_index("rep")
    c = lax.rem(me, 2)
    y = lax.rem(me // 2, 2)
    z = me // 4
    up, down = me + 4, me - 4
    across, twin = me + 2 - 4 * y, me + 1 - 2 * c
    has_up, has_down = z < depth - 1, z > 0

    def block(zz, yy, cc):
        return (zz * 2 + yy) * 2 + cc

    def copy(tile, sem, target):
        return pltpu.make_async_remote_copy(
            src_ref=held.at[tile], dst_ref=held.at[tile], send_sem=sem,
            recv_sem=recv_sem.at[tile], device_id={"rep": target}, device_id_type=MESH)

    def arrived(tile):
        copy(tile, c_sem.at[0], twin).wait_recv()

    def unit(zz, u):
        if u == tiles:
            return block(zz, 1 - y, c) * tiles + last
        return block(zz, y, c) * tiles + u

    def up_copy(zz, u):
        return copy(unit(zz, u), z_sem.at[zz * (tiles + 1) + u], up)

    def down_copy(zz, u):
        spot = jnp.where(zz == z, depth, zz)
        return copy(unit(zz, u), z_sem.at[spot * (tiles + 1) + u], down)

    def y_copy(zz, u):
        return copy(unit(zz, u), y_sem.at[zz * tiles + u], across)

    def c_copy(zz, yy, u):
        return copy(block(zz, yy, c) * tiles + u, c_sem.at[(zz * 2 + yy) * tiles + u], twin)

    barrier = pltpu.get_barrier_semaphore()
    pl.semaphore_signal(barrier, inc=1, device_id={"rep": across}, device_id_type=MESH)
    pl.semaphore_signal(barrier, inc=1, device_id={"rep": twin}, device_id_type=MESH)

    @pl.when(has_up)
    def _():
        pl.semaphore_signal(barrier, inc=1, device_id={"rep": up}, device_id_type=MESH)

    @pl.when(has_down)
    def _():
        pl.semaphore_signal(barrier, inc=1, device_id={"rep": down}, device_id_type=MESH)

    fetch = pltpu.make_async_copy(adj_ref, adj.at[pl.ds(0, stored)], adj_sem)
    fetch.start()
    projected = jnp.dot(
        feat_ref[...].astype(jnp.bfloat16), weight_ref[...], preferred_element_type=jnp.float32
    ).astype(jnp.bfloat16)
    for u in range(tiles):
        held[me * tiles + u] = projected[u * rows:(u + 1) * rows]
    adj[stored] = jnp.zeros((rows, rows), jnp.bfloat16)
    pl.semaphore_wait(barrier, 2 + has_up.astype(jnp.int32) + has_down.astype(jnp.int32))

    y_copy(z, last).start()
    for u in range(tiles):
        @pl.when(has_up)
        def _():
            up_copy(z, u).start()

        @pl.when(has_down)
        def _():
            down_copy(z, u).start()

        if u != last:
            y_copy(z, u).start()
    for u in range(tiles):
        c_copy(z, y, u).start()

    out_ref[...] = jnp.zeros_like(out_ref)

    def consume(b):
        for pair in range(tiles // 2):
            first = b * tiles + 2 * pair
            right = jnp.concatenate([held[first], held[first + 1]], axis=0)
            left = jnp.concatenate([
                jnp.concatenate([adj[slot_ref[r * every + first]],
                                 adj[slot_ref[r * every + first + 1]]], axis=1)
                for r in range(tiles)], axis=0)
            out_ref[...] += jnp.dot(left, right, preferred_element_type=jnp.float32)

    def take(zz, yy, flip):
        b = block(zz, yy, c + flip * (1 - 2 * c))

        @pl.when(flip == 1)
        def _():
            for u in range(tiles):
                arrived(b * tiles + u)

        consume(b)

    arrived(unit(z, tiles))

    @pl.when(has_up)
    def _():
        up_copy(z, tiles).start()

    @pl.when(has_down)
    def _():
        down_copy(z, tiles).start()

    c_copy(z, 1 - y, last).start()
    fetch.wait()

    @pl.loop(0, 2)
    def _(flip):
        take(z, y, flip)

    @pl.loop(1, depth + 1)
    def _(hop):
        for u in range(tiles + 1):
            for sign in (-1, 1):
                zz = z + sign * hop

                @pl.when((zz >= 0) & (zz < depth))
                def _():
                    arrived(unit(zz, u))
                    if sign == -1:
                        @pl.when(has_up)
                        def _():
                            up_copy(zz, u).start()
                    else:
                        @pl.when(has_down)
                        def _():
                            down_copy(zz, u).start()
                    if u < last:
                        y_copy(zz, u).start()
                    if u == tiles:
                        c_copy(zz, 1 - y, last).start()
                    else:
                        c_copy(zz, y, u).start()
            if u < last:
                for sign in (-1, 1):
                    zz = z + sign * (hop - 1)
                    fresh = (zz >= 0) & (zz < depth)
                    if sign == 1:
                        fresh = fresh & (hop > 1)

                    @pl.when(fresh)
                    def _():
                        arrived(block(zz, 1 - y, c) * tiles + u)
                        c_copy(zz, 1 - y, u).start()

        @pl.loop(0, 8)
        def _(i):
            flip = lax.rem(i, 2)
            side = lax.rem(i // 2, 2)
            older = i // 4
            distance = hop - older
            zz = z + distance * (2 * side - 1)
            yy = y + older * (1 - 2 * y)

            @pl.when((zz >= 0) & (zz < depth) & ((distance > 0) | (side == 0)))
            def _():
                take(zz, yy, flip)

    @pl.loop(0, depth)
    def _(zz):
        for u in range(tiles + 1):
            @pl.when(has_up & (zz <= z))
            def _():
                up_copy(zz, u).wait_send()

            @pl.when(has_down & (zz >= z))
            def _():
                down_copy(zz, u).wait_send()
        for u in range(tiles):
            if u < last:
                y_copy(zz, u).wait_send()
            c_copy(zz, 0, u).wait_send()
            c_copy(zz, 1, u).wait_send()
    y_copy(z, last).wait_send()


def shards(rep, features, weight, adjacency, col_tiles):
    tiles, stored, rows, _ = adjacency.shape
    width = features.shape[1]
    every = rep * tiles
    depth = rep // 4
    total = tiles * stored
    spots = jnp.arange(total, dtype=jnp.int32).reshape(tiles, stored)
    named = col_tiles[:, :, None] == jnp.arange(every, dtype=jnp.int32)
    slots = total + jnp.sum(jnp.where(named, spots[:, :, None] - total, 0), axis=1)
    summed = pl.pallas_call(
        functools.partial(kernel, depth, tiles),
        out_shape=jax.ShapeDtypeStruct(features.shape, jnp.float32),
        in_specs=[
            pl.BlockSpec(memory_space=pltpu.VMEM),
            pl.BlockSpec(memory_space=pltpu.VMEM),
            pl.BlockSpec(memory_space=pltpu.SMEM),
            pl.BlockSpec(memory_space=pl.ANY),
        ],
        out_specs=pl.BlockSpec(memory_space=pltpu.VMEM),
        scratch_shapes=[
            pltpu.VMEM((every, rows, width), jnp.bfloat16),
            pltpu.VMEM((total + 1, rows, rows), jnp.bfloat16),
            pltpu.SemaphoreType.DMA,
            pltpu.SemaphoreType.DMA((every,)),
            pltpu.SemaphoreType.DMA(((depth + 1) * (tiles + 1),)),
            pltpu.SemaphoreType.DMA((depth * tiles,)),
            pltpu.SemaphoreType.DMA((depth * 2 * tiles,)),
        ],
        compiler_params=pltpu.CompilerParams(
            collective_id=0, has_side_effects=True, vmem_limit_bytes=56 * 1024 * 1024),
        cost_estimate=pl.CostEstimate(
            flops=2 * tiles * every * rows * rows * width,
            bytes_accessed=total * rows * rows * 2, transcendentals=0),
    )(features, weight, slots.reshape(-1), adjacency.reshape(total, rows, rows))
    return jnp.maximum(summed, 0.0)


def solution(mesh):
    return jax.shard_map(
        functools.partial(shards, mesh.shape["rep"]),
        mesh=mesh,
        in_specs=(
            P(("groups", "rep"), None),
            P(),
            P(("groups", "rep"), None, None, None),
            P(("groups", "rep"), None),
        ),
        out_specs=P(("groups", "rep"), None),
        check_vma=False,
    )
```

```python
import functools

import jax
import jax.numpy as jnp
from jax import lax
from jax.experimental import pallas as pl
from jax.experimental.pallas import tpu as pltpu
from jax.sharding import PartitionSpec as P

MESH = pl.DeviceIdType.MESH


def kernel(depth, tiles, feat_hbm, weight_hbm, cols_hbm, adj_hbm, out_ref,
           held, adj, feat, weight, cols, table, slot_ref,
           in_sem, recv_sem, z_sem, y_sem, c_sem):
    rep = depth * 4
    every = rep * tiles
    rows = held.shape[1]
    stored = cols_hbm.shape[1]
    total = tiles * stored
    last = tiles - 1
    me = lax.axis_index("rep")
    c = lax.rem(me, 2)
    y = lax.rem(me // 2, 2)
    z = me // 4
    up, down = me + 4, me - 4
    across, twin = me + 2 - 4 * y, me + 1 - 2 * c
    has_up, has_down = z < depth - 1, z > 0

    def block(zz, yy, cc):
        return (zz * 2 + yy) * 2 + cc

    def copy(tile, sem, target):
        return pltpu.make_async_remote_copy(
            src_ref=held.at[tile], dst_ref=held.at[tile], send_sem=sem,
            recv_sem=recv_sem.at[tile], device_id={"rep": target}, device_id_type=MESH)

    def arrived(tile):
        copy(tile, c_sem.at[0], twin).wait_recv()

    def unit(zz, u):
        if u == tiles:
            return block(zz, 1 - y, c) * tiles + last
        return block(zz, y, c) * tiles + u

    def up_copy(zz, u):
        return copy(unit(zz, u), z_sem.at[zz * (tiles + 1) + u], up)

    def down_copy(zz, u):
        spot = jnp.where(zz == z, depth, zz)
        return copy(unit(zz, u), z_sem.at[spot * (tiles + 1) + u], down)

    def y_copy(zz, u):
        return copy(unit(zz, u), y_sem.at[zz * tiles + u], across)

    def c_copy(zz, yy, u):
        return copy(block(zz, yy, c) * tiles + u, c_sem.at[(zz * 2 + yy) * tiles + u], twin)

    barrier = pltpu.get_barrier_semaphore()
    pl.semaphore_signal(barrier, inc=1, device_id={"rep": across}, device_id_type=MESH)
    pl.semaphore_signal(barrier, inc=1, device_id={"rep": twin}, device_id_type=MESH)

    @pl.when(has_up)
    def _():
        pl.semaphore_signal(barrier, inc=1, device_id={"rep": up}, device_id_type=MESH)

    @pl.when(has_down)
    def _():
        pl.semaphore_signal(barrier, inc=1, device_id={"rep": down}, device_id_type=MESH)

    def fetch(source, target, n):
        return pltpu.make_async_copy(source, target, in_sem.at[n])

    fetch_weight = fetch(weight_hbm, weight, 0)
    fetch_cols = fetch(cols_hbm, cols, 1)
    fetch_adj = fetch(adj_hbm, adj.at[pl.ds(0, total)], 2)
    fetch_feat = [fetch(feat_hbm.at[pl.ds(u * rows, rows)], feat.at[pl.ds(u * rows, rows)], 3 + u)
                  for u in range(tiles)]
    fetch_weight.start()
    order = [last] + list(range(last))
    for u in order:
        fetch_feat[u].start()
    fetch_cols.start()
    fetch_adj.start()

    def project(u):
        fetch_feat[u].wait()
        held[me * tiles + u] = jnp.dot(
            feat[u * rows:(u + 1) * rows].astype(jnp.bfloat16), weight[...],
            preferred_element_type=jnp.float32).astype(jnp.bfloat16)

    fetch_weight.wait()
    project(last)
    pl.semaphore_wait(barrier, 2 + has_up.astype(jnp.int32) + has_down.astype(jnp.int32))
    y_copy(z, last).start()
    for u in range(tiles):
        if u != last:
            project(u)

        @pl.when(has_up)
        def _():
            up_copy(z, u).start()

        @pl.when(has_down)
        def _():
            down_copy(z, u).start()

        if u != last:
            y_copy(z, u).start()
        c_copy(z, y, u).start()

    fetch_cols.wait()
    named = cols[...]
    lane = lax.broadcasted_iota(jnp.int32, (tiles, every), 1)
    base = lax.broadcasted_iota(jnp.int32, (tiles, every), 0) * stored
    slots = jnp.full((tiles, every), total, jnp.int32)
    for k in range(stored):
        slots = jnp.where(named[:, k:k + 1] == lane, base + k, slots)
    table[...] = slots
    publish = fetch(table, slot_ref, 1)
    publish.start()
    adj[total] = jnp.zeros((rows, rows), jnp.bfloat16)
    out_ref[...] = jnp.zeros_like(out_ref)

    def consume(b):
        for pair in range(tiles // 2):
            first = b * tiles + 2 * pair
            right = jnp.concatenate([held[first], held[first + 1]], axis=0)
            left = jnp.concatenate([
                jnp.concatenate([adj[slot_ref[r, first]],
                                 adj[slot_ref[r, first + 1]]], axis=1)
                for r in range(tiles)], axis=0)
            out_ref[...] += jnp.dot(left, right, preferred_element_type=jnp.float32)

    def take(zz, yy, flip):
        b = block(zz, yy, c + flip * (1 - 2 * c))

        @pl.when(flip == 1)
        def _():
            for u in range(tiles):
                arrived(b * tiles + u)

        consume(b)

    arrived(unit(z, tiles))

    @pl.when(has_up)
    def _():
        up_copy(z, tiles).start()

    @pl.when(has_down)
    def _():
        down_copy(z, tiles).start()

    c_copy(z, 1 - y, last).start()
    publish.wait()
    fetch_adj.wait()

    @pl.loop(0, 2)
    def _(flip):
        take(z, y, flip)

    @pl.loop(1, depth + 1)
    def _(hop):
        for u in range(tiles + 1):
            for sign in (-1, 1):
                zz = z + sign * hop

                @pl.when((zz >= 0) & (zz < depth))
                def _():
                    arrived(unit(zz, u))
                    if sign == -1:
                        @pl.when(has_up)
                        def _():
                            up_copy(zz, u).start()
                    else:
                        @pl.when(has_down)
                        def _():
                            down_copy(zz, u).start()
                    if u < last:
                        y_copy(zz, u).start()
                    if u == tiles:
                        c_copy(zz, 1 - y, last).start()
                    else:
                        c_copy(zz, y, u).start()
            if u < last:
                for sign in (-1, 1):
                    zz = z + sign * (hop - 1)
                    fresh = (zz >= 0) & (zz < depth)
                    if sign == 1:
                        fresh = fresh & (hop > 1)

                    @pl.when(fresh)
                    def _():
                        arrived(block(zz, 1 - y, c) * tiles + u)
                        c_copy(zz, 1 - y, u).start()

        @pl.loop(0, 8)
        def _(i):
            flip = lax.rem(i, 2)
            side = lax.rem(i // 2, 2)
            older = i // 4
            distance = hop - older
            zz = z + distance * (2 * side - 1)
            yy = y + older * (1 - 2 * y)

            @pl.when((zz >= 0) & (zz < depth) & ((distance > 0) | (side == 0)))
            def _():
                take(zz, yy, flip)

    @pl.loop(0, depth)
    def _(zz):
        for u in range(tiles + 1):
            @pl.when(has_up & (zz <= z))
            def _():
                up_copy(zz, u).wait_send()

            @pl.when(has_down & (zz >= z))
            def _():
                down_copy(zz, u).wait_send()
        for u in range(tiles):
            if u < last:
                y_copy(zz, u).wait_send()
            c_copy(zz, 0, u).wait_send()
            c_copy(zz, 1, u).wait_send()
    y_copy(z, last).wait_send()


def shards(rep, features, weight, adjacency, col_tiles):
    tiles, stored, rows, _ = adjacency.shape
    width = features.shape[1]
    every = rep * tiles
    depth = rep // 4
    total = tiles * stored
    summed = pl.pallas_call(
        functools.partial(kernel, depth, tiles),
        out_shape=jax.ShapeDtypeStruct(features.shape, jnp.float32),
        in_specs=[pl.BlockSpec(memory_space=pl.ANY)] * 4,
        out_specs=pl.BlockSpec(memory_space=pltpu.VMEM),
        scratch_shapes=[
            pltpu.VMEM((every, rows, width), jnp.bfloat16),
            pltpu.VMEM((total + 1, rows, rows), jnp.bfloat16),
            pltpu.VMEM(features.shape, jnp.float32),
            pltpu.VMEM(weight.shape, jnp.bfloat16),
            pltpu.VMEM(col_tiles.shape, jnp.int32),
            pltpu.VMEM((tiles, every), jnp.int32),
            pltpu.SMEM((tiles, every), jnp.int32),
            pltpu.SemaphoreType.DMA((3 + tiles,)),
            pltpu.SemaphoreType.DMA((every,)),
            pltpu.SemaphoreType.DMA(((depth + 1) * (tiles + 1),)),
            pltpu.SemaphoreType.DMA((depth * tiles,)),
            pltpu.SemaphoreType.DMA((depth * 2 * tiles,)),
        ],
        compiler_params=pltpu.CompilerParams(
            collective_id=0, has_side_effects=True,
            vmem_limit_bytes=56 * 1024 * 1024),
        cost_estimate=pl.CostEstimate(
            flops=2 * tiles * every * rows * rows * width,
            bytes_accessed=total * rows * rows * 2, transcendentals=0),
    )(features, weight, col_tiles, adjacency.reshape(total, rows, rows))
    return jnp.maximum(summed, 0.0)


def solution(mesh):
    return jax.shard_map(
        functools.partial(shards, mesh.shape["rep"]),
        mesh=mesh,
        in_specs=(
            P(("groups", "rep"), None),
            P(),
            P(("groups", "rep"), None, None, None),
            P(("groups", "rep"), None),
        ),
        out_specs=P(("groups", "rep"), None),
        check_vma=False,
    )
```

```python
import functools

import jax
import jax.numpy as jnp
from jax import lax
from jax.experimental import pallas as pl
from jax.experimental.pallas import tpu as pltpu
from jax.sharding import PartitionSpec as P

MESH = pl.DeviceIdType.MESH


def kernel(depth, tiles, feat_hbm, weight_hbm, cols_hbm, adj_hbm, out_ref,
           held, adj, feat, weight, cols, table, slot_ref,
           in_sem, recv_sem, z_sem, y_sem, c_sem):
    rep = depth * 4
    every = rep * tiles
    rows = held.shape[1]
    stored = cols_hbm.shape[1]
    total = tiles * stored
    last = tiles - 1
    me = lax.axis_index("rep")
    c = lax.rem(me, 2)
    y = lax.rem(me // 2, 2)
    z = me // 4
    up, down = me + 4, me - 4
    across, twin = me + 2 - 4 * y, me + 1 - 2 * c
    has_up, has_down = z < depth - 1, z > 0

    def block(zz, yy, cc):
        return (zz * 2 + yy) * 2 + cc

    def copy(tile, sem, target):
        return pltpu.make_async_remote_copy(
            src_ref=held.at[tile], dst_ref=held.at[tile], send_sem=sem,
            recv_sem=recv_sem.at[tile], device_id={"rep": target}, device_id_type=MESH)

    def arrived(tile):
        copy(tile, c_sem.at[0], twin).wait_recv()

    def unit(zz, u):
        if u == tiles:
            return block(zz, 1 - y, c) * tiles + last
        return block(zz, y, c) * tiles + u

    def up_copy(zz, u):
        return copy(unit(zz, u), z_sem.at[zz * (tiles + 1) + u], up)

    def down_copy(zz, u):
        spot = jnp.where(zz == z, depth, zz)
        return copy(unit(zz, u), z_sem.at[spot * (tiles + 1) + u], down)

    def y_copy(zz, u):
        return copy(unit(zz, u), y_sem.at[zz * tiles + u], across)

    def c_copy(zz, yy, u):
        return copy(block(zz, yy, c) * tiles + u, c_sem.at[(zz * 2 + yy) * tiles + u], twin)

    barrier = pltpu.get_barrier_semaphore()
    pl.semaphore_signal(barrier, inc=1, device_id={"rep": across}, device_id_type=MESH)
    pl.semaphore_signal(barrier, inc=1, device_id={"rep": twin}, device_id_type=MESH)

    @pl.when(has_up)
    def _():
        pl.semaphore_signal(barrier, inc=1, device_id={"rep": up}, device_id_type=MESH)

    @pl.when(has_down)
    def _():
        pl.semaphore_signal(barrier, inc=1, device_id={"rep": down}, device_id_type=MESH)

    def fetch(source, target, n):
        return pltpu.make_async_copy(source, target, in_sem.at[n])

    fetch_weight = fetch(weight_hbm, weight, 0)
    fetch_cols = fetch(cols_hbm, cols, 1)
    fetch_adj = fetch(adj_hbm, adj.at[pl.ds(0, total)], 2)
    fetch_feat = [fetch(feat_hbm.at[pl.ds(u * rows, rows)], feat.at[pl.ds(u * rows, rows)], 3 + u)
                  for u in range(tiles)]
    fetch_weight.start()
    order = [last] + list(range(last))
    for u in order:
        fetch_feat[u].start()
    fetch_cols.start()
    fetch_adj.start()

    def project(u):
        fetch_feat[u].wait()
        held[me * tiles + u] = jnp.dot(
            feat[u * rows:(u + 1) * rows].astype(jnp.bfloat16), weight[...],
            preferred_element_type=jnp.float32).astype(jnp.bfloat16)

    fetch_weight.wait()
    project(last)
    pl.semaphore_wait(barrier, 2 + has_up.astype(jnp.int32) + has_down.astype(jnp.int32))
    y_copy(z, last).start()
    for u in range(tiles):
        if u != last:
            project(u)

        @pl.when(has_up)
        def _():
            up_copy(z, u).start()

        @pl.when(has_down)
        def _():
            down_copy(z, u).start()

        if u != last:
            y_copy(z, u).start()
        c_copy(z, y, u).start()

    fetch_cols.wait()
    named = cols[...]
    lane = lax.broadcasted_iota(jnp.int32, (tiles, every), 1)
    base = lax.broadcasted_iota(jnp.int32, (tiles, every), 0) * stored
    slots = jnp.full((tiles, every), total, jnp.int32)
    for k in range(stored):
        slots = jnp.where(named[:, k:k + 1] == lane, base + k, slots)
    table[...] = slots
    publish = fetch(table, slot_ref, 1)
    publish.start()
    adj[total] = jnp.zeros((rows, rows), jnp.bfloat16)
    out_ref[...] = jnp.zeros_like(out_ref)

    def consume(b):
        for pair in range(tiles // 2):
            first = b * tiles + 2 * pair
            right = jnp.concatenate([held[first], held[first + 1]], axis=0)
            left = jnp.concatenate([
                jnp.concatenate([adj[slot_ref[r, first]],
                                 adj[slot_ref[r, first + 1]]], axis=1)
                for r in range(tiles)], axis=0)
            out_ref[...] += jnp.dot(left, right, preferred_element_type=jnp.float32)

    def take(zz, yy, flip):
        b = block(zz, yy, c + flip * (1 - 2 * c))

        @pl.when(flip == 1)
        def _():
            for u in range(tiles):
                arrived(b * tiles + u)

        consume(b)

    arrived(unit(z, tiles))

    @pl.when(has_up)
    def _():
        up_copy(z, tiles).start()

    @pl.when(has_down)
    def _():
        down_copy(z, tiles).start()

    c_copy(z, 1 - y, last).start()
    publish.wait()
    fetch_adj.wait()

    @pl.loop(0, 2)
    def _(flip):
        take(z, y, flip)

    @pl.loop(1, depth + 1)
    def _(hop):
        for u in range(tiles + 1):
            for sign in (-1, 1):
                zz = z + sign * hop

                @pl.when((zz >= 0) & (zz < depth))
                def _():
                    arrived(unit(zz, u))
                    if sign == -1:
                        @pl.when(has_up)
                        def _():
                            up_copy(zz, u).start()
                    else:
                        @pl.when(has_down)
                        def _():
                            down_copy(zz, u).start()
                    if u < last:
                        y_copy(zz, u).start()
                    if u == tiles:
                        c_copy(zz, 1 - y, last).start()
                    else:
                        c_copy(zz, y, u).start()
            if u < last:
                for sign in (-1, 1):
                    zz = z + sign * (hop - 1)
                    fresh = (zz >= 0) & (zz < depth)
                    if sign == 1:
                        fresh = fresh & (hop > 1)

                    @pl.when(fresh)
                    def _():
                        arrived(block(zz, 1 - y, c) * tiles + u)
                        c_copy(zz, 1 - y, u).start()

        @pl.loop(0, 8)
        def _(i):
            flip = lax.rem(i, 2)
            side = lax.rem(i // 2, 2)
            older = i // 4
            distance = hop - older
            zz = z + distance * (2 * side - 1)
            yy = y + older * (1 - 2 * y)

            @pl.when((zz >= 0) & (zz < depth) & ((distance > 0) | (side == 0)))
            def _():
                take(zz, yy, flip)

    @pl.loop(0, depth)
    def _(zz):
        for u in range(tiles + 1):
            @pl.when(has_up & (zz <= z))
            def _():
                up_copy(zz, u).wait_send()

            @pl.when(has_down & (zz >= z))
            def _():
                down_copy(zz, u).wait_send()
        for u in range(tiles):
            if u < last:
                y_copy(zz, u).wait_send()
            c_copy(zz, 0, u).wait_send()
            c_copy(zz, 1, u).wait_send()
    y_copy(z, last).wait_send()


def shards(rep, features, weight, adjacency, col_tiles):
    tiles, stored, rows, _ = adjacency.shape
    width = features.shape[1]
    every = rep * tiles
    depth = rep // 4
    total = tiles * stored
    summed = pl.pallas_call(
        functools.partial(kernel, depth, tiles),
        out_shape=jax.ShapeDtypeStruct(features.shape, jnp.float32),
        in_specs=[pl.BlockSpec(memory_space=pl.ANY)] * 4,
        out_specs=pl.BlockSpec(memory_space=pltpu.VMEM),
        scratch_shapes=[
            pltpu.VMEM((every, rows, width), jnp.bfloat16),
            pltpu.VMEM((total + 1, rows, rows), jnp.bfloat16),
            pltpu.VMEM(features.shape, jnp.float32),
            pltpu.VMEM(weight.shape, jnp.bfloat16),
            pltpu.VMEM(col_tiles.shape, jnp.int32),
            pltpu.VMEM((tiles, every), jnp.int32),
            pltpu.SMEM((tiles, every), jnp.int32),
            pltpu.SemaphoreType.DMA((3 + tiles,)),
            pltpu.SemaphoreType.DMA((every,)),
            pltpu.SemaphoreType.DMA(((depth + 1) * (tiles + 1),)),
            pltpu.SemaphoreType.DMA((depth * tiles,)),
            pltpu.SemaphoreType.DMA((depth * 2 * tiles,)),
        ],
        compiler_params=pltpu.CompilerParams(
            collective_id=0, has_side_effects=True,
            vmem_limit_bytes=53 * 1024 * 1024),
        cost_estimate=pl.CostEstimate(
            flops=2 * tiles * every * rows * rows * width,
            bytes_accessed=total * rows * rows * 2, transcendentals=0),
    )(features, weight, col_tiles, adjacency.reshape(total, rows, rows))
    return jnp.maximum(summed, 0.0)


def solution(mesh):
    return jax.shard_map(
        functools.partial(shards, mesh.shape["rep"]),
        mesh=mesh,
        in_specs=(
            P(("groups", "rep"), None),
            P(),
            P(("groups", "rep"), None, None, None),
            P(("groups", "rep"), None),
        ),
        out_specs=P(("groups", "rep"), None),
        check_vma=False,
    )
```

```python
import functools

import jax
import jax.numpy as jnp
from jax import lax
from jax.experimental import pallas as pl
from jax.experimental.pallas import tpu as pltpu
from jax.sharding import PartitionSpec as P

MESH = pl.DeviceIdType.MESH


def kernel(depth, tiles, feat_hbm, weight_hbm, cols_hbm, adj_hbm, out_ref,
           held, adj, feat, weight, cols, table, slot_ref,
           in_sem, recv_sem, z_sem, y_sem, c_sem):
    rep = depth * 4
    every = rep * tiles
    rows = held.shape[1]
    stored = cols_hbm.shape[1]
    total = tiles * stored
    last = tiles - 1
    me = lax.axis_index("rep")
    c = lax.rem(me, 2)
    y = lax.rem(me // 2, 2)
    z = me // 4
    up, down = me + 4, me - 4
    across, twin = me + 2 - 4 * y, me + 1 - 2 * c
    has_up, has_down = z < depth - 1, z > 0

    def block(zz, yy, cc):
        return (zz * 2 + yy) * 2 + cc

    def copy(tile, sem, target):
        return pltpu.make_async_remote_copy(
            src_ref=held.at[tile], dst_ref=held.at[tile], send_sem=sem,
            recv_sem=recv_sem.at[tile], device_id={"rep": target}, device_id_type=MESH)

    def arrived(tile):
        copy(tile, c_sem.at[0], twin).wait_recv()

    def unit(zz, u):
        if u == tiles:
            return block(zz, 1 - y, c) * tiles + last
        return block(zz, y, c) * tiles + u

    def up_copy(zz, u):
        return copy(unit(zz, u), z_sem.at[zz * (tiles + 1) + u], up)

    def down_copy(zz, u):
        spot = jnp.where(zz == z, depth, zz)
        return copy(unit(zz, u), z_sem.at[spot * (tiles + 1) + u], down)

    def y_copy(zz, u):
        return copy(unit(zz, u), y_sem.at[zz * tiles + u], across)

    def c_copy(zz, yy, u):
        return copy(block(zz, yy, c) * tiles + u, c_sem.at[(zz * 2 + yy) * tiles + u], twin)

    barrier = pltpu.get_barrier_semaphore()
    pl.semaphore_signal(barrier, inc=1, device_id={"rep": across}, device_id_type=MESH)
    pl.semaphore_signal(barrier, inc=1, device_id={"rep": twin}, device_id_type=MESH)

    @pl.when(has_up)
    def _():
        pl.semaphore_signal(barrier, inc=1, device_id={"rep": up}, device_id_type=MESH)

    @pl.when(has_down)
    def _():
        pl.semaphore_signal(barrier, inc=1, device_id={"rep": down}, device_id_type=MESH)

    def fetch(source, target, n):
        return pltpu.make_async_copy(source, target, in_sem.at[n])

    fetch_weight = fetch(weight_hbm, weight, 0)
    fetch_cols = fetch(cols_hbm, cols, 1)
    fetch_adj = fetch(adj_hbm, adj.at[pl.ds(0, total)], 2)
    fetch_feat = [fetch(feat_hbm.at[pl.ds(u * rows, rows)], feat.at[pl.ds(u * rows, rows)], 3 + u)
                  for u in range(tiles)]
    fetch_weight.start()
    order = [last] + list(range(last))
    for u in order:
        fetch_feat[u].start()
    fetch_cols.start()
    fetch_adj.start()

    def project(u):
        fetch_feat[u].wait()
        held[me * tiles + u] = jnp.dot(
            feat[u * rows:(u + 1) * rows].astype(jnp.bfloat16), weight[...],
            preferred_element_type=jnp.float32).astype(jnp.bfloat16)

    fetch_weight.wait()
    project(last)
    pl.semaphore_wait(barrier, 2 + has_up.astype(jnp.int32) + has_down.astype(jnp.int32))
    y_copy(z, last).start()
    for u in range(tiles):
        if u != last:
            project(u)

        @pl.when(has_up)
        def _():
            up_copy(z, u).start()

        @pl.when(has_down)
        def _():
            down_copy(z, u).start()

        if u != last:
            y_copy(z, u).start()
        c_copy(z, y, u).start()

    fetch_cols.wait()
    named = cols[...]
    lane = lax.broadcasted_iota(jnp.int32, (tiles, every), 1)
    base = lax.broadcasted_iota(jnp.int32, (tiles, every), 0) * stored
    slots = jnp.full((tiles, every), total, jnp.int32)
    for k in range(stored):
        slots = jnp.where(named[:, k:k + 1] == lane, base + k, slots)
    table[...] = slots
    publish = fetch(table, slot_ref, 1)
    publish.start()
    adj[total] = jnp.zeros((rows, rows), jnp.bfloat16)
    out_ref[...] = jnp.zeros_like(out_ref)

    def consume(b):
        first = b * tiles
        right = held[pl.ds(first, tiles)].reshape(tiles * rows, -1)
        left = jnp.concatenate([
            jnp.concatenate([adj[slot_ref[r, first + u]] for u in range(tiles)], axis=1)
            for r in range(tiles)], axis=0)
        out_ref[...] += jnp.dot(left, right, preferred_element_type=jnp.float32)

    def take(zz, yy, flip):
        b = block(zz, yy, c + flip * (1 - 2 * c))

        @pl.when(flip == 1)
        def _():
            for u in range(tiles):
                arrived(b * tiles + u)

        consume(b)

    arrived(unit(z, tiles))

    @pl.when(has_up)
    def _():
        up_copy(z, tiles).start()

    @pl.when(has_down)
    def _():
        down_copy(z, tiles).start()

    c_copy(z, 1 - y, last).start()
    publish.wait()
    fetch_adj.wait()

    @pl.loop(0, 2)
    def _(flip):
        take(z, y, flip)

    @pl.loop(1, depth + 1)
    def _(hop):
        for u in range(tiles + 1):
            for sign in (-1, 1):
                zz = z + sign * hop

                @pl.when((zz >= 0) & (zz < depth))
                def _():
                    arrived(unit(zz, u))
                    if sign == -1:
                        @pl.when(has_up)
                        def _():
                            up_copy(zz, u).start()
                    else:
                        @pl.when(has_down)
                        def _():
                            down_copy(zz, u).start()
                    if u < last:
                        y_copy(zz, u).start()
                    if u == tiles:
                        c_copy(zz, 1 - y, last).start()
                    else:
                        c_copy(zz, y, u).start()
            if u < last:
                for sign in (-1, 1):
                    zz = z + sign * (hop - 1)
                    fresh = (zz >= 0) & (zz < depth)
                    if sign == 1:
                        fresh = fresh & (hop > 1)

                    @pl.when(fresh)
                    def _():
                        arrived(block(zz, 1 - y, c) * tiles + u)
                        c_copy(zz, 1 - y, u).start()

        @pl.loop(0, 8)
        def _(i):
            flip = lax.rem(i, 2)
            side = lax.rem(i // 2, 2)
            older = i // 4
            distance = hop - older
            zz = z + distance * (2 * side - 1)
            yy = y + older * (1 - 2 * y)

            @pl.when((zz >= 0) & (zz < depth) & ((distance > 0) | (side == 0)))
            def _():
                take(zz, yy, flip)

    @pl.loop(0, depth)
    def _(zz):
        for u in range(tiles + 1):
            @pl.when(has_up & (zz <= z))
            def _():
                up_copy(zz, u).wait_send()

            @pl.when(has_down & (zz >= z))
            def _():
                down_copy(zz, u).wait_send()
        for u in range(tiles):
            if u < last:
                y_copy(zz, u).wait_send()
            c_copy(zz, 0, u).wait_send()
            c_copy(zz, 1, u).wait_send()
    y_copy(z, last).wait_send()


def shards(rep, features, weight, adjacency, col_tiles):
    tiles, stored, rows, _ = adjacency.shape
    width = features.shape[1]
    every = rep * tiles
    depth = rep // 4
    total = tiles * stored
    summed = pl.pallas_call(
        functools.partial(kernel, depth, tiles),
        out_shape=jax.ShapeDtypeStruct(features.shape, jnp.float32),
        in_specs=[pl.BlockSpec(memory_space=pl.ANY)] * 4,
        out_specs=pl.BlockSpec(memory_space=pltpu.VMEM),
        scratch_shapes=[
            pltpu.VMEM((every, rows, width), jnp.bfloat16),
            pltpu.VMEM((total + 1, rows, rows), jnp.bfloat16),
            pltpu.VMEM(features.shape, jnp.float32),
            pltpu.VMEM(weight.shape, jnp.bfloat16),
            pltpu.VMEM(col_tiles.shape, jnp.int32),
            pltpu.VMEM((tiles, every), jnp.int32),
            pltpu.SMEM((tiles, every), jnp.int32),
            pltpu.SemaphoreType.DMA((3 + tiles,)),
            pltpu.SemaphoreType.DMA((every,)),
            pltpu.SemaphoreType.DMA(((depth + 1) * (tiles + 1),)),
            pltpu.SemaphoreType.DMA((depth * tiles,)),
            pltpu.SemaphoreType.DMA((depth * 2 * tiles,)),
        ],
        compiler_params=pltpu.CompilerParams(
            collective_id=0, has_side_effects=True,
            vmem_limit_bytes=53 * 1024 * 1024),
        cost_estimate=pl.CostEstimate(
            flops=2 * tiles * every * rows * rows * width,
            bytes_accessed=total * rows * rows * 2, transcendentals=0),
    )(features, weight, col_tiles, adjacency.reshape(total, rows, rows))
    return jnp.maximum(summed, 0.0)


def solution(mesh):
    return jax.shard_map(
        functools.partial(shards, mesh.shape["rep"]),
        mesh=mesh,
        in_specs=(
            P(("groups", "rep"), None),
            P(),
            P(("groups", "rep"), None, None, None),
            P(("groups", "rep"), None),
        ),
        out_specs=P(("groups", "rep"), None),
        check_vma=False,
    )
```
